32 devices in a mesh: tm: 4 (over y, core), space: 8 (over z, x).
Axes of the slice: x: 2, y: 2, z: 4, core: 2. Of those that a mesh axis runs over, the one named last changes fastest.
Arguments:
- rhs_state: float32 [4, 4, 128, 1280], P('tm', None, 'space'), may hold values from -12 to 12
- rhs_obs: float32 [4, 4, 4, 128, 1280], P('tm', None, None, 'space'), may hold values from -12 to 12
- wind_east: float32 [4, 4, 4, 128, 1280], P('tm', None, None, 'space'), may hold values from -0.45 to 0.45
- wind_north: float32 [4, 4, 4, 128, 1280], P('tm', None, None, 'space'), may hold values from -0.45 to 0.45
- model_var: float32 [4, 4, 128, 1280], P('tm', None, 'space'), may hold values from 0.5 to 2
- obs_var: float32 [4, 4, 4, 128, 1280], P('tm', None, None, 'space'), may hold values from 0.5 to 2
- obs_mask: int32 [4, 4, 4, 128, 1280], P('tm', None, None, 'space'), may hold values 0 or 1
Outputs:
- dual_model: float32 [4, 4, 128, 1280], P('tm', None, 'space')
- dual_obs: float32 [4, 4, 4, 128, 1280], P('tm', None, None, 'space')
- increment: float32 [4, 4, 128, 1280], P('tm', None, 'space')
The draws below stay inside these ranges and needn't reach their ends.
All inputs are finite; a program needn't handle non-finite values. No bound on the sum of `obs_mask` on one device may be relied on, other than what follows from the above.
Results may differ from the reference program's by a relative error of at most 0.0001.
Values sent between devices are 32-bit elements; how exact they have to be, the bound alone decides.
A program may use at most 64 MiB of HBM per device.

```python
import math
import jax
import jax.numpy as jnp

LEV = 4
NLON = 1280
STEPS = 4
ITERS = 2
WINDOWS = 4
NLAT = 128


def band_field(key, lead):
    shape = lead + (LEV, NLAT, NLON)
    base = jnp.clip(jax.random.normal(key, shape, jnp.float32), -5.0, 5.0)
    rows = jnp.arange(NLAT, dtype=jnp.float32) / NLAT
    spans = jnp.arange(WINDOWS, dtype=jnp.float32) / WINDOWS
    factor = (0.6 + 1.2 * rows)[:, None] * jnp.ones((NLON,), jnp.float32)[None, :]
    factor = factor.reshape((1,) * len(lead) + (1, NLAT, NLON))
    window_factor = (0.7 + 0.6 * spans).reshape((WINDOWS,) + (1,) * (len(lead) + 2))
    return (base * factor * window_factor).astype(jnp.float32)


def draw_rhs_state(key, part):
    key = jax.random.fold_in(key, 11)
    return band_field(key, (WINDOWS,))


def draw_rhs_obs(key, part):
    key = jax.random.fold_in(key, 23)
    return band_field(key, (WINDOWS, STEPS))


def with_ends(drawn, stream_key, low, top_value):
    longest = drawn.shape.index(max(drawn.shape))
    spots = []
    for shift in (0, 1):
        where = [jax.random.randint(jax.random.fold_in(stream_key, axis), (), 0, length) for axis, length in enumerate(drawn.shape)]
        where[longest] = (where[longest] + shift) % drawn.shape[longest]
        spots.append(tuple(where))
    return drawn.at[spots[0]].set(low).at[spots[1]].set(top_value)


def block_levels(stream_key, extent, shards, least, largest):
    def one(axis_at, shards_of):
        steps = jax.random.uniform(jax.random.fold_in(jax.random.fold_in(stream_key, 6), axis_at), (shards_of,), jnp.float32, least / len(shards), largest / len(shards))
        return jnp.repeat(jnp.exp(steps), extent[axis_at] // shards_of).reshape((-1,) + (1,) * (len(extent) - axis_at - 1))

    level = one(*shards[0])
    for cut in shards[1:]:
        level = level * one(*cut)
    return level


def setup_inputs(seed: int = 0) -> dict:
    streams_of = jax.random.split(jax.random.key(seed), 8)
    return {
        "rhs_state": draw_rhs_state(jax.random.fold_in(streams_of[7], 71), 0),
        "rhs_obs": draw_rhs_obs(jax.random.fold_in(streams_of[7], 71), 0),
        "wind_east": jnp.clip(jax.random.uniform(streams_of[2], (WINDOWS, STEPS, LEV, NLAT, NLON), jnp.float32, -0.45, 0.45) * block_levels(streams_of[2], (WINDOWS, STEPS, LEV, NLAT, NLON), ((0, 4), (3, 8)), -0.4, 0.0), -0.45, 0.45),
        "wind_north": jnp.clip(jax.random.uniform(streams_of[3], (WINDOWS, STEPS, LEV, NLAT, NLON), jnp.float32, -0.45, 0.45) * block_levels(streams_of[3], (WINDOWS, STEPS, LEV, NLAT, NLON), ((0, 4), (3, 8)), -0.4, 0.0), -0.45, 0.45),
        "model_var": jnp.clip(jnp.exp(math.log(2.0) - 1.3862944 * jax.random.uniform(streams_of[4], (WINDOWS, LEV, NLAT, NLON), jnp.float32) ** block_levels(streams_of[4], (WINDOWS, LEV, NLAT, NLON), ((0, 4), (2, 8)), -0.2, 0.2)), 0.5, 2.0),
        "obs_var": jnp.clip(jnp.exp(math.log(2.0) - 1.3862944 * jax.random.uniform(streams_of[5], (WINDOWS, STEPS, LEV, NLAT, NLON), jnp.float32) ** block_levels(streams_of[5], (WINDOWS, STEPS, LEV, NLAT, NLON), ((0, 4), (3, 8)), -0.2, 0.2)), 0.5, 2.0),
        "obs_mask": with_ends((jax.random.randint(streams_of[6], (WINDOWS, STEPS, LEV, NLAT, NLON), 0, 3) < 1).astype(jnp.int32), jax.random.fold_in(streams_of[6], 1), 0, 1),
    }


KAPPA = 0.12


def pad_rows(field):
    widths = [(0, 0)] * (field.ndim - 2) + [(1, 1), (0, 0)]
    return jnp.pad(field, widths)


def forward_step(padded, east_c, north_c):
    cells = padded[..., 1:-1, :]
    upper = padded[..., 2:, :]
    lower = padded[..., :-2, :]
    after = jnp.roll(cells, -1, -1)
    before = jnp.roll(cells, 1, -1)
    return (cells - 0.5 * east_c * (after - before) - 0.5 * north_c * (upper - lower)
            + KAPPA * (after + before + upper + lower - 4.0 * cells))


def adjoint_step(padded, weighted, east_c):
    cells = padded[..., 1:-1, :]
    flux = east_c * cells
    along = jnp.roll(KAPPA * cells - 0.5 * flux, 1, -1) + jnp.roll(KAPPA * cells + 0.5 * flux, -1, -1)
    across = (KAPPA * padded[..., :-2, :] - 0.5 * weighted[..., :-2, :]
              + KAPPA * padded[..., 2:, :] + 0.5 * weighted[..., 2:, :])
    return (1.0 - 4.0 * KAPPA) * cells + along + across


def reference(rhs_state, rhs_obs, wind_east, wind_north, model_var, obs_var, obs_mask):
    mask = obs_mask.astype(jnp.float32)

    def operator(lam, dual, delta):
        state = delta
        observed = []
        for j in range(STEPS):
            state = forward_step(pad_rows(state), wind_east[:, j], wind_north[:, j])
            observed.append(mask[:, j] * state)
        ends = jnp.concatenate([jnp.zeros_like(state[:1]), state[:-1]], 0)
        out_lam = model_var * lam + delta - ends
        out_dual = obs_var * dual + jnp.stack(observed, 1)
        nexts = jnp.concatenate([lam[1:], jnp.zeros_like(lam[:1])], 0)
        adjoint = -nexts
        for j in reversed(range(STEPS)):
            adjoint = adjoint + mask[:, j] * dual[:, j]
            adjoint = adjoint_step(pad_rows(adjoint), pad_rows(wind_north[:, j] * adjoint), wind_east[:, j])
        return out_lam, out_dual, lam + adjoint

    res = (rhs_state, rhs_obs, jnp.zeros_like(rhs_state))
    sol = (jnp.zeros_like(rhs_state), jnp.zeros_like(rhs_obs), jnp.zeros_like(rhs_state))
    for step in range(ITERS):
        image = operator(*res)
        inner = sum(jnp.sum(p * q) for p, q in zip(res, image))
        square = sum(jnp.sum(q * q) for q in image)
        alpha = inner / square
        sol = tuple(s + alpha * p for s, p in zip(sol, res))
        res = tuple(p - alpha * q for p, q in zip(res, image))
    return sol[0], sol[1], sol[2]
```

```python
import functools

import jax
import jax.numpy as jnp
from jax import lax
from jax.experimental import pallas as pl
from jax.experimental.pallas import tpu as pltpu
from jax.sharding import PartitionSpec as P

KAPPA = 0.12
MESH = pl.DeviceIdType.MESH


def kernel(
    ntm, nsp,
    rs_h, ro_h, we_h, wn_h, mv_h, ov_h, mk_h,
    zdx_h, coef_ref,
    rs, ro, we, wn, mv, ov, mk,
    zl, zdx, u, t1, t2, st,
    lam_next, zl_next, u_next,
    acc, stage_lo, stage_hi, recv_lo, recv_hi,
    part, part_tm, part_sp,
    load_sem, slo_sem, shi_sem, rlo_sem, rhi_sem, tms_sem, tmr_sem,
    ptm_s, ptm_r, psp_s, psp_r, out_sem,
):
    steps, lev, rows, nlon = ro.shape
    last = rows - 1
    tm = lax.axis_index("tm")
    sp = lax.axis_index("space")
    has_lo, has_hi = sp > 0, sp < nsp - 1
    has_prev, has_next = tm > 0, tm < ntm - 1

    loads = {}

    def load(name, src, dst):
        copy = pltpu.make_async_copy(src, dst, load_sem.at[len(loads)])
        copy.start()
        loads[name] = copy

    load("rs", rs_h, rs)
    load("mv", mv_h, mv)
    for j in reversed(range(steps)):
        load(("mk", j), mk_h.at[j], mk.at[j])
        load(("ro", j), ro_h.at[j], ro.at[j])
        load(("wn", j), wn_h.at[j], wn.at[j])
        load(("we", j), we_h.at[j], we.at[j])
    for j in reversed(range(steps)):
        load(("ov", j), ov_h.at[j], ov.at[j])

    barrier = pltpu.get_barrier_semaphore()
    for d in range(1, ntm):
        pl.semaphore_signal(barrier, inc=1, device_id=(lax.rem(tm + d, ntm), sp), device_id_type=MESH)
    for d in range(1, nsp):
        pl.semaphore_signal(barrier, inc=1, device_id=(tm, lax.rem(sp + d, nsp)), device_id_type=MESH)
    pl.semaphore_wait(barrier, ntm + nsp - 2)

    def tm_copy(i, src, dst, device):
        return pltpu.make_async_remote_copy(
            src_ref=src, dst_ref=dst, send_sem=tms_sem.at[i], recv_sem=tmr_sem.at[i],
            device_id=(device, sp), device_id_type=MESH,
        )

    def tm_send(i, src, dst):
        @pl.when(has_prev)
        def _():
            tm_copy(i, src, dst, tm - 1).start()

    def tm_recv(i, src, dst):
        @pl.when(has_next)
        def _():
            tm_copy(i, src, dst, tm + 1).wait_recv()

    def to_lo(slot, device):
        return pltpu.make_async_remote_copy(
            src_ref=stage_lo.at[slot], dst_ref=recv_hi.at[slot],
            send_sem=slo_sem.at[slot], recv_sem=rhi_sem.at[slot],
            device_id=(tm, device), device_id_type=MESH,
        )

    def to_hi(slot, device):
        return pltpu.make_async_remote_copy(
            src_ref=stage_hi.at[slot], dst_ref=recv_lo.at[slot],
            send_sem=shi_sem.at[slot], recv_sem=rlo_sem.at[slot],
            device_id=(tm, device), device_id_type=MESH,
        )

    row = lax.broadcasted_iota(jnp.int32, (rows, nlon), 0)

    def down(x):
        return jnp.where(row == 0, 0.0, pltpu.roll(x, 1, 0))

    def up(x):
        return jnp.where(row == last, 0.0, pltpu.roll(x, rows - 1, 0))

    def before(x):
        return pltpu.roll(x, 1, 1)

    def after(x):
        return pltpu.roll(x, nlon - 1, 1)

    def fold(x):
        total = x[0:8]
        for i in range(8, rows, 8):
            total = total + x[i:i + 8]
        return total

    def levels(body):
        lax.fori_loop(0, lev, lambda l, c: (body(l), c)[1], 0)

    loads["rs"].wait()
    tm_send(0, rs, lam_next)
    loads["mv"].wait()

    def _(l):
        z = mv[l] * rs[l]
        zl[l] = z
        acc[0, l] = fold(z * rs[l])
        acc[1, l] = fold(z * z)
        acc[2, l] = jnp.zeros((8, nlon), jnp.float32)
        acc[3, l] = jnp.zeros((8, nlon), jnp.float32)
    levels(_)
    tm_send(1, zl, zl_next)

    @pl.when(jnp.logical_not(has_next))
    def _():
        lam_next[...] = jnp.zeros_like(lam_next)
        zl_next[...] = jnp.zeros_like(zl_next)

    def mask(j, l):
        return mk[j, l].astype(jnp.float32)

    for name in ("mk", "ro", "wn", "we"):
        loads[name, steps - 1].wait()
    tm_recv(0, rs, lam_next)

    def _(l):
        t1[l] = mask(steps - 1, l) * ro[steps - 1, l] - lam_next[l]
    levels(_)

    def send_adjoint(slot, t, j):
        def _(l):
            lo = t[l, 0:1, :]
            hi = t[l, last:rows, :]
            stage_lo[slot, pl.ds(l, 1), :] = KAPPA * lo + 0.5 * (wn[j, l, 0:1, :] * lo)
            stage_hi[slot, pl.ds(l, 1), :] = KAPPA * hi - 0.5 * (wn[j, l, last:rows, :] * hi)
        for l in range(lev):
            _(l)
        start(slot)

    def send_forward(slot, s):
        for l in range(lev):
            stage_lo[slot, pl.ds(l, 1), :] = s[l, 0:1, :]
            stage_hi[slot, pl.ds(l, 1), :] = s[l, last:rows, :]
        start(slot)

    def start(slot):
        @pl.when(has_lo)
        def _():
            to_lo(slot, sp - 1).start()

        @pl.when(has_hi)
        def _():
            to_hi(slot, sp + 1).start()

    def finish(slot, t, j=None):
        @pl.when(has_lo)
        def _():
            to_hi(slot, sp - 1).wait_recv()
            for l in range(lev):
                got = recv_lo[slot, pl.ds(l, 1), :]
                if j is not None:
                    got = (KAPPA + 0.5 * wn[j, l, 0:1, :]) * got
                t[l, 0:1, :] = t[l, 0:1, :] + got

        @pl.when(has_hi)
        def _():
            to_lo(slot, sp + 1).wait_recv()
            for l in range(lev):
                got = recv_hi[slot, pl.ds(l, 1), :]
                if j is not None:
                    got = (KAPPA - 0.5 * wn[j, l, last:rows, :]) * got
                t[l, last:rows, :] = t[l, last:rows, :] + got

    def transposed(t, j, l):
        x = t[l]
        k = KAPPA * x
        e = 0.5 * (we[j, l] * x)
        n = 0.5 * (wn[j, l] * x)
        return (1.0 - 4.0 * KAPPA) * x + before(k - e) + after(k + e) + down(k - n) + up(k + n)

    def adjoint1(j):
        if j > 0:
            def _(l):
                t1[l] = transposed(t1, j, l) + mask(j - 1, l) * ro[j - 1, l]
        else:
            def _(l):
                zdx[l] = transposed(t1, j, l) + rs[l]
        levels(_)

    def inject2(j, l):
        z = ov[j, l] * ro[j, l]
        acc[0, l] += fold(z * ro[j, l])
        acc[1, l] += fold(z * z)
        return mask(j, l) * z

    def adjoint2(j):
        if j > 0:
            def _(l):
                t2[l] = transposed(t2, j, l) + inject2(j - 1, l)
        else:
            def _(l):
                t2[l] = transposed(t2, j, l) + zl[l]
        levels(_)

    def observed(j, l, s):
        z = ov[j, l] * ro[j, l]
        w = ov[j, l] * z + mask(j, l) * s
        acc[2, l] += fold(z * w)
        acc[3, l] += fold(w * w)

    def forward(src, j):
        def _(l):
            x = src[l]
            if j > 0:
                observed(j - 1, l, x)
            else:
                acc[1, l] += fold(x * x)
                u[l] = mv[l] * zl[l] + x
            e, w = after(x), before(x)
            n, s = up(x), down(x)
            st[l] = (
                x
                - 0.5 * (we[j, l] * (e - w))
                - 0.5 * (wn[j, l] * (n - s))
                + KAPPA * (e + w + n + s - 4.0 * x)
            )
        levels(_)

    def start2():
        for j in reversed(range(steps)):
            loads["ov", j].wait()
        tm_recv(1, zl, zl_next)

        def _(l):
            t2[l] = inject2(steps - 1, l) - zl_next[l]
        levels(_)

    def round2(q):
        j = steps - 1 - q
        if q == 0:
            start2()
        else:
            finish(2 * steps + q - 1, t2)
        if q < steps:
            send_adjoint(2 * steps + q, t2, j)
            adjoint2(j)

    def own_window():
        @pl.when(jnp.logical_not(has_prev))
        def _():
            def _(l):
                acc[2, l] += fold(zl[l] * u[l])
                acc[3, l] += fold(u[l] * u[l])
            levels(_)

    def increments():
        def _(l):
            acc[2, l] += fold(zdx[l] * t2[l])
            acc[3, l] += fold(t2[l] * t2[l])
        levels(_)

    lag = steps // 2
    for r in range(2 * steps):
        if r < steps:
            j = steps - 1 - r
            send_adjoint(r, t1, j)
            if j > 0:
                for name in ("mk", "ro", "wn", "we"):
                    loads[name, j - 1].wait()
            adjoint1(j)
            target = t1 if j > 0 else zdx
            weight = None
        else:
            j = r - steps
            src = zdx if j == 0 else st
            send_forward(r, src)
            if j == 0:
                out = pltpu.make_async_copy(zdx, zdx_h, out_sem)
                out.start()
            forward(src, j)
            if j == 0:
                tm_send(2, u, u_next)
            target, weight = st, j
        if lag <= r <= lag + steps:
            round2(r - lag)
        if r == lag + steps:
            increments()
        if r == 2 * steps - 1:
            own_window()
            tm_recv(2, u, u_next)
        finish(r, target, weight)

    def _(l):
        observed(steps - 1, l, st[l])
    levels(_)

    @pl.when(has_next)
    def _():
        def _(l):
            w = u_next[l] - st[l]
            acc[2, l] += fold(zl_next[l] * w)
            acc[3, l] += fold(w * w)
        levels(_)

    for i in range(4):
        total = acc[i, 0]
        for l in range(1, lev):
            total = total + acc[i, l]
        lanes = total[:, 0:128]
        for c in range(128, nlon, 128):
            lanes = lanes + total[:, c:c + 128]
        part[0, i:i + 1, :] = jnp.sum(lanes, axis=0, keepdims=True)
    part[0, 4:8, :] = jnp.zeros((4, 128), jnp.float32)

    def gather(count, slots, sends, recvs, device, src):
        copies = [
            pltpu.make_async_remote_copy(
                src_ref=src, dst_ref=slots.at[d - 1],
                send_sem=sends.at[d - 1], recv_sem=recvs.at[d - 1],
                device_id=device(d), device_id_type=MESH,
            )
            for d in range(1, count)
        ]
        for copy in copies:
            copy.start()
        total = src[...]
        for d, copy in enumerate(copies):
            copy.wait_recv()
            total = total + slots[d]
        return total, copies

    total, copies1 = gather(
        ntm, part_tm, ptm_s, ptm_r, lambda d: (lax.rem(tm + d, ntm), sp), part.at[0]
    )
    part[1] = total
    total, copies2 = gather(
        nsp, part_sp, psp_s, psp_r, lambda d: (tm, lax.rem(sp + d, nsp)), part.at[1]
    )
    sums = jnp.broadcast_to(jnp.sum(total, axis=1, keepdims=True), (8, 128))
    n, d, e, f = (sums[i:i + 1, :] for i in range(4))
    first = n / d
    second = first * (first * e - d) / (d - 2.0 * first * e + first * first * f)
    coef_ref[0:1, :] = first + second
    coef_ref[1:2, :] = -(first * second)
    coef_ref[2:8, :] = jnp.zeros((6, 128), jnp.float32)

    for copy in copies1 + copies2:
        copy.wait_send()
    for slot in range(3 * steps):
        @pl.when(has_lo)
        def _(slot=slot):
            to_lo(slot, sp - 1).wait_send()

        @pl.when(has_hi)
        def _(slot=slot):
            to_hi(slot, sp + 1).wait_send()

    @pl.when(has_prev)
    def _():
        tm_copy(0, rs, lam_next, tm - 1).wait_send()
        tm_copy(1, zl, zl_next, tm - 1).wait_send()
        tm_copy(2, u, u_next, tm - 1).wait_send()
    out.wait()


def on_device(ntm, nsp, *args):
    rhs_state, rhs_obs, wind_east, wind_north, model_var, obs_var, obs_mask = (a[0] for a in args)
    steps, lev, rows, nlon = rhs_obs.shape
    f32 = jnp.float32
    field = pltpu.VMEM((lev, rows, nlon), f32)
    fields = pltpu.VMEM((steps, lev, rows, nlon), f32)
    slots = 3 * steps
    halo = pltpu.VMEM((slots, lev, nlon), f32)
    dma = pltpu.SemaphoreType.DMA
    hbm = pl.BlockSpec(memory_space=pl.ANY)
    zdx, coef = pl.pallas_call(
        functools.partial(kernel, ntm, nsp),
        out_shape=(
            jax.ShapeDtypeStruct((lev, rows, nlon), f32),
            jax.ShapeDtypeStruct((8, 128), f32),
        ),
        in_specs=[hbm] * 7,
        out_specs=(hbm, pl.BlockSpec(memory_space=pltpu.VMEM)),
        scratch_shapes=[
            field, fields, fields, fields, field, fields,
            pltpu.VMEM((steps, lev, rows, nlon), jnp.int32),
            field, field, field, field, field, field,
            field, field, field,
            pltpu.VMEM((4, lev, 8, nlon), f32), halo, halo, halo, halo,
            pltpu.VMEM((2, 8, 128), f32),
            pltpu.VMEM((ntm - 1, 8, 128), f32),
            pltpu.VMEM((nsp - 1, 8, 128), f32),
            dma((2 + 5 * steps,)), dma((slots,)), dma((slots,)), dma((slots,)), dma((slots,)),
            dma((3,)), dma((3,)),
            dma((ntm - 1,)), dma((ntm - 1,)), dma((nsp - 1,)), dma((nsp - 1,)), dma,
        ],
        compiler_params=pltpu.CompilerParams(
            collective_id=0, has_side_effects=True, vmem_limit_bytes=56 * 1024 * 1024
        ),
    )(rhs_state, rhs_obs, wind_east, wind_north, model_var, obs_var, obs_mask)
    both, cross = coef[0, 0], coef[1, 0]
    return (
        ((both + cross * model_var) * rhs_state)[None],
        ((both + cross * obs_var) * rhs_obs)[None],
        (cross * zdx)[None],
    )


def solution(mesh):
    flat = P("tm", None, "space", None)
    deep = P("tm", None, None, "space", None)
    return jax.shard_map(
        functools.partial(on_device, mesh.shape["tm"], mesh.shape["space"]),
        mesh=mesh,
        in_specs=(flat, deep, deep, deep, flat, deep, deep),
        out_specs=(flat, deep, flat),
        check_vma=False,
    )
```

```python
import functools

import jax
import jax.numpy as jnp
from jax import lax
from jax.experimental import pallas as pl
from jax.experimental.pallas import tpu as pltpu
from jax.sharding import PartitionSpec as P

KAPPA = 0.12
MESH = pl.DeviceIdType.MESH


def kernel(
    ntm, nsp,
    rs_h, ro_h, we_h, wn_h, mv_h, ov_h, mk_h,
    zdx_h, coef_ref,
    rs, ro, we, wn, mv, ov, mk,
    zl, zdx, u, t1, t2, st,
    lam_next, zl_next, u_next,
    acc, stage_lo, stage_hi, recv_lo, recv_hi,
    part, part_tm, part_sp,
    load_sem, slo_sem, shi_sem, rlo_sem, rhi_sem, tms_sem, tmr_sem,
    ptm_s, ptm_r, psp_s, psp_r, out_sem,
):
    steps, lev, rows, nlon = ro.shape
    last = rows - 1
    tm = lax.axis_index("tm")
    sp = lax.axis_index("space")
    has_lo, has_hi = sp > 0, sp < nsp - 1
    has_prev, has_next = tm > 0, tm < ntm - 1

    loads = {}

    def load(name, src, dst):
        copy = pltpu.make_async_copy(src, dst, load_sem.at[len(loads)])
        copy.start()
        loads[name] = copy

    load("rs", rs_h, rs)
    load("mv", mv_h, mv)
    for j in reversed(range(steps)):
        load(("mk", j), mk_h.at[j], mk.at[j])
        load(("ro", j), ro_h.at[j], ro.at[j])
        load(("wn", j), wn_h.at[j], wn.at[j])
        load(("we", j), we_h.at[j], we.at[j])
    for j in reversed(range(steps)):
        load(("ov", j), ov_h.at[j], ov.at[j])

    barrier = pltpu.get_barrier_semaphore()
    for d in range(1, ntm):
        pl.semaphore_signal(barrier, inc=1, device_id=(lax.rem(tm + d, ntm), sp), device_id_type=MESH)
    for d in range(1, nsp):
        pl.semaphore_signal(barrier, inc=1, device_id=(tm, lax.rem(sp + d, nsp)), device_id_type=MESH)
    pl.semaphore_wait(barrier, ntm + nsp - 2)

    def tm_copy(i, src, dst, device):
        return pltpu.make_async_remote_copy(
            src_ref=src, dst_ref=dst, send_sem=tms_sem.at[i], recv_sem=tmr_sem.at[i],
            device_id=(device, sp), device_id_type=MESH,
        )

    def tm_send(i, src, dst):
        @pl.when(has_prev)
        def _():
            tm_copy(i, src, dst, tm - 1).start()

    def tm_recv(i, src, dst):
        @pl.when(has_next)
        def _():
            tm_copy(i, src, dst, tm + 1).wait_recv()

    def to_lo(slot, device):
        return pltpu.make_async_remote_copy(
            src_ref=stage_lo.at[slot], dst_ref=recv_hi.at[slot],
            send_sem=slo_sem.at[slot], recv_sem=rhi_sem.at[slot],
            device_id=(tm, device), device_id_type=MESH,
        )

    def to_hi(slot, device):
        return pltpu.make_async_remote_copy(
            src_ref=stage_hi.at[slot], dst_ref=recv_lo.at[slot],
            send_sem=shi_sem.at[slot], recv_sem=rlo_sem.at[slot],
            device_id=(tm, device), device_id_type=MESH,
        )

    row = lax.broadcasted_iota(jnp.int32, (rows, nlon), 0)

    def down(x):
        return jnp.where(row == 0, 0.0, pltpu.roll(x, 1, 0))

    def up(x):
        return jnp.where(row == last, 0.0, pltpu.roll(x, rows - 1, 0))

    def before(x):
        return pltpu.roll(x, 1, 1)

    def after(x):
        return pltpu.roll(x, nlon - 1, 1)

    def fold(x):
        total = x[0:8]
        for i in range(8, rows, 8):
            total = total + x[i:i + 8]
        return total

    def levels(body):
        lax.fori_loop(0, lev, lambda l, c: (body(l), c)[1], 0)

    loads["rs"].wait()
    tm_send(0, rs, lam_next)
    loads["mv"].wait()

    def _(l):
        z = mv[l] * rs[l]
        zl[l] = z
        acc[0, l] = fold(z * rs[l])
        acc[1, l] = fold(z * z)
        acc[2, l] = jnp.zeros((8, nlon), jnp.float32)
        acc[3, l] = jnp.zeros((8, nlon), jnp.float32)
    levels(_)
    tm_send(1, zl, zl_next)

    @pl.when(jnp.logical_not(has_next))
    def _():
        lam_next[...] = jnp.zeros_like(lam_next)
        zl_next[...] = jnp.zeros_like(zl_next)

    def mask(j, l):
        return mk[j, l].astype(jnp.float32)

    for name in ("mk", "ro", "wn", "we"):
        loads[name, steps - 1].wait()
    tm_recv(0, rs, lam_next)

    def _(l):
        t1[l] = mask(steps - 1, l) * ro[steps - 1, l] - lam_next[l]
    levels(_)

    def send_adjoint(slot, t, j):
        def _(l):
            lo = t[l, 0:1, :]
            hi = t[l, last:rows, :]
            stage_lo[slot, pl.ds(l, 1), :] = KAPPA * lo + 0.5 * (wn[j, l, 0:1, :] * lo)
            stage_hi[slot, pl.ds(l, 1), :] = KAPPA * hi - 0.5 * (wn[j, l, last:rows, :] * hi)
        for l in range(lev):
            _(l)
        start(slot)

    def send_forward(slot, s):
        for l in range(lev):
            stage_lo[slot, pl.ds(l, 1), :] = s[l, 0:1, :]
            stage_hi[slot, pl.ds(l, 1), :] = s[l, last:rows, :]
        start(slot)

    def start(slot):
        @pl.when(has_lo)
        def _():
            to_lo(slot, sp - 1).start()

        @pl.when(has_hi)
        def _():
            to_hi(slot, sp + 1).start()

    def finish(slot, t, j=None):
        @pl.when(has_lo)
        def _():
            to_hi(slot, sp - 1).wait_recv()
            for l in range(lev):
                got = recv_lo[slot, pl.ds(l, 1), :]
                if j is not None:
                    got = (KAPPA + 0.5 * wn[j, l, 0:1, :]) * got
                t[l, 0:1, :] = t[l, 0:1, :] + got

        @pl.when(has_hi)
        def _():
            to_lo(slot, sp + 1).wait_recv()
            for l in range(lev):
                got = recv_hi[slot, pl.ds(l, 1), :]
                if j is not None:
                    got = (KAPPA - 0.5 * wn[j, l, last:rows, :]) * got
                t[l, last:rows, :] = t[l, last:rows, :] + got

    def transposed(t, j, l):
        x = t[l]
        k = KAPPA * x
        e = 0.5 * (we[j, l] * x)
        n = 0.5 * (wn[j, l] * x)
        return (1.0 - 4.0 * KAPPA) * x + before(k - e) + after(k + e) + down(k - n) + up(k + n)

    def adjoint1(j):
        if j > 0:
            def _(l):
                t1[l] = transposed(t1, j, l) + mask(j - 1, l) * ro[j - 1, l]
        else:
            def _(l):
                zdx[l] = transposed(t1, j, l) + rs[l]
        levels(_)

    def inject2(j, l):
        z = ov[j, l] * ro[j, l]
        acc[0, l] += fold(z * ro[j, l])
        acc[1, l] += fold(z * z)
        return mask(j, l) * z

    def adjoint2(j):
        if j > 0:
            def _(l):
                t2[l] = transposed(t2, j, l) + inject2(j - 1, l)
        else:
            def _(l):
                t2[l] = transposed(t2, j, l) + zl[l]
        levels(_)

    def observed(j, l, s):
        z = ov[j, l] * ro[j, l]
        w = ov[j, l] * z + mask(j, l) * s
        acc[2, l] += fold(z * w)
        acc[3, l] += fold(w * w)

    def forward(src, j):
        def _(l):
            x = src[l]
            if j > 0:
                observed(j - 1, l, x)
            else:
                acc[1, l] += fold(x * x)
                u[l] = mv[l] * zl[l] + x
            e, w = after(x), before(x)
            n, s = up(x), down(x)
            st[l] = (
                x
                - 0.5 * (we[j, l] * (e - w))
                - 0.5 * (wn[j, l] * (n - s))
                + KAPPA * (e + w + n + s - 4.0 * x)
            )
        levels(_)

    def start2():
        for j in reversed(range(steps)):
            loads["ov", j].wait()
        tm_recv(1, zl, zl_next)

        def _(l):
            t2[l] = inject2(steps - 1, l) - zl_next[l]
        levels(_)

    def round2(q):
        j = steps - 1 - q
        if q == 0:
            start2()
        else:
            finish(2 * steps + q - 1, t2)
        if q < steps:
            send_adjoint(2 * steps + q, t2, j)
            adjoint2(j)

    def own_window():
        @pl.when(jnp.logical_not(has_prev))
        def _():
            def _(l):
                acc[2, l] += fold(zl[l] * u[l])
                acc[3, l] += fold(u[l] * u[l])
            levels(_)

    def increments():
        def _(l):
            acc[2, l] += fold(zdx[l] * t2[l])
            acc[3, l] += fold(t2[l] * t2[l])
        levels(_)

    lag = steps // 2
    for r in range(2 * steps):
        if r < steps:
            j = steps - 1 - r
            send_adjoint(r, t1, j)
            if j > 0:
                for name in ("mk", "ro", "wn", "we"):
                    loads[name, j - 1].wait()
            adjoint1(j)
            target = t1 if j > 0 else zdx
            weight = None
        else:
            j = r - steps
            src = zdx if j == 0 else st
            send_forward(r, src)
            if j == 0:
                out = pltpu.make_async_copy(zdx, zdx_h, out_sem)
                out.start()
            forward(src, j)
            if j == 0:
                tm_send(2, u, u_next)
            target, weight = st, j
        if lag <= r <= lag + steps:
            round2(r - lag)
        if r == lag + steps:
            increments()
        if r == 2 * steps - 1:
            own_window()
            tm_recv(2, u, u_next)
        finish(r, target, weight)

    def _(l):
        observed(steps - 1, l, st[l])
    levels(_)

    @pl.when(has_next)
    def _():
        def _(l):
            w = u_next[l] - st[l]
            acc[2, l] += fold(zl_next[l] * w)
            acc[3, l] += fold(w * w)
        levels(_)

    for i in range(4):
        total = acc[i, 0]
        for l in range(1, lev):
            total = total + acc[i, l]
        lanes = total[:, 0:128]
        for c in range(128, nlon, 128):
            lanes = lanes + total[:, c:c + 128]
        part[0, i:i + 1, :] = jnp.sum(lanes, axis=0, keepdims=True)
    part[0, 4:8, :] = jnp.zeros((4, 128), jnp.float32)

    def gather(count, slots, sends, recvs, device, src):
        copies = [
            pltpu.make_async_remote_copy(
                src_ref=src, dst_ref=slots.at[d - 1],
                send_sem=sends.at[d - 1], recv_sem=recvs.at[d - 1],
                device_id=device(d), device_id_type=MESH,
            )
            for d in range(1, count)
        ]
        for copy in copies:
            copy.start()
        total = src[...]
        for d, copy in enumerate(copies):
            copy.wait_recv()
            total = total + slots[d]
        return total, copies

    total, copies1 = gather(
        ntm, part_tm, ptm_s, ptm_r, lambda d: (lax.rem(tm + d, ntm), sp), part.at[0]
    )
    part[1] = total
    total, copies2 = gather(
        nsp, part_sp, psp_s, psp_r, lambda d: (tm, lax.rem(sp + d, nsp)), part.at[1]
    )
    sums = jnp.broadcast_to(jnp.sum(total, axis=1, keepdims=True), (8, 128))
    n, d, e, f = (sums[i:i + 1, :] for i in range(4))
    first = n / d
    second = first * (first * e - d) / (d - 2.0 * first * e + first * first * f)
    coef_ref[0:1, :] = first + second
    coef_ref[1:2, :] = -(first * second)
    coef_ref[2:8, :] = jnp.zeros((6, 128), jnp.float32)

    for copy in copies1 + copies2:
        copy.wait_send()
    for slot in range(3 * steps):
        @pl.when(has_lo)
        def _(slot=slot):
            to_lo(slot, sp - 1).wait_send()

        @pl.when(has_hi)
        def _(slot=slot):
            to_hi(slot, sp + 1).wait_send()

    @pl.when(has_prev)
    def _():
        tm_copy(0, rs, lam_next, tm - 1).wait_send()
        tm_copy(1, zl, zl_next, tm - 1).wait_send()
        tm_copy(2, u, u_next, tm - 1).wait_send()
    out.wait()


def combine(coef, rs, ro, mv, ov, zdx, lam_h, mu_h, dx_h, lam, mu, dx, sem):
    steps, lev, rows, nlon = ro.shape
    both = jnp.broadcast_to(coef[0:1, 0:1], (rows, nlon))
    cross = jnp.broadcast_to(coef[1:2, 0:1], (rows, nlon))
    copies = []

    def put(body, src, dst):
        lax.fori_loop(0, lev, lambda l, c: (body(l), c)[1], 0)
        copy = pltpu.make_async_copy(src, dst, sem.at[len(copies)])
        copy.start()
        copies.append(copy)

    for j in range(steps):
        def _(l, j=j):
            mu[j, l] = (both + cross * ov[j, l]) * ro[j, l]
        put(_, mu.at[j], mu_h.at[j])

    def _(l):
        lam[l] = (both + cross * mv[l]) * rs[l]
    put(_, lam, lam_h)

    def _(l):
        dx[l] = cross * zdx[l]
    put(_, dx, dx_h)
    for copy in copies:
        copy.wait()


def on_device(ntm, nsp, *args):
    rhs_state, rhs_obs, wind_east, wind_north, model_var, obs_var, obs_mask = (a[0] for a in args)
    steps, lev, rows, nlon = rhs_obs.shape
    f32 = jnp.float32
    field = pltpu.VMEM((lev, rows, nlon), f32)
    fields = pltpu.VMEM((steps, lev, rows, nlon), f32)
    slots = 3 * steps
    halo = pltpu.VMEM((slots, lev, nlon), f32)
    dma = pltpu.SemaphoreType.DMA
    hbm = pl.BlockSpec(memory_space=pl.ANY)
    zdx, coef = pl.pallas_call(
        functools.partial(kernel, ntm, nsp),
        out_shape=(
            jax.ShapeDtypeStruct((lev, rows, nlon), f32),
            jax.ShapeDtypeStruct((8, 128), f32),
        ),
        in_specs=[hbm] * 7,
        out_specs=(hbm, pl.BlockSpec(memory_space=pltpu.VMEM)),
        scratch_shapes=[
            field, fields, fields, fields, field, fields,
            pltpu.VMEM((steps, lev, rows, nlon), jnp.int32),
            field, field, field, field, field, field,
            field, field, field,
            pltpu.VMEM((4, lev, 8, nlon), f32), halo, halo, halo, halo,
            pltpu.VMEM((2, 8, 128), f32),
            pltpu.VMEM((ntm - 1, 8, 128), f32),
            pltpu.VMEM((nsp - 1, 8, 128), f32),
            dma((2 + 5 * steps,)), dma((slots,)), dma((slots,)), dma((slots,)), dma((slots,)),
            dma((3,)), dma((3,)),
            dma((ntm - 1,)), dma((ntm - 1,)), dma((nsp - 1,)), dma((nsp - 1,)), dma,
        ],
        compiler_params=pltpu.CompilerParams(
            collective_id=0, has_side_effects=True, vmem_limit_bytes=52 * 1024 * 1024
        ),
    )(rhs_state, rhs_obs, wind_east, wind_north, model_var, obs_var, obs_mask)
    vmem = pl.BlockSpec(memory_space=pltpu.VMEM)
    lam, mu, dx = pl.pallas_call(
        combine,
        out_shape=(
            jax.ShapeDtypeStruct((lev, rows, nlon), f32),
            jax.ShapeDtypeStruct((steps, lev, rows, nlon), f32),
            jax.ShapeDtypeStruct((lev, rows, nlon), f32),
        ),
        in_specs=[vmem] * 6,
        out_specs=(hbm, hbm, hbm),
        scratch_shapes=[field, fields, field, dma((steps + 2,))],
        compiler_params=pltpu.CompilerParams(vmem_limit_bytes=16 * 1024 * 1024),
    )(coef, rhs_state, rhs_obs, model_var, obs_var, zdx)
    return lam[None], mu[None], dx[None]


def solution(mesh):
    flat = P("tm", None, "space", None)
    deep = P("tm", None, None, "space", None)
    return jax.shard_map(
        functools.partial(on_device, mesh.shape["tm"], mesh.shape["space"]),
        mesh=mesh,
        in_specs=(flat, deep, deep, deep, flat, deep, deep),
        out_specs=(flat, deep, flat),
        check_vma=False,
    )
```

```python
import functools

import jax
import jax.numpy as jnp
from jax import lax
from jax.experimental import pallas as pl
from jax.experimental.pallas import tpu as pltpu
from jax.sharding import PartitionSpec as P

KAPPA = 0.12
MESH = pl.DeviceIdType.MESH


def kernel(
    ntm, nsp,
    rs_h, ro_h, we_h, wn_h, mv_h, ov_h, mk_h,
    zdx_h, coef_ref,
    rs, ro, we, wn, mv, ov, mk,
    zl, zdx, u, t1, t2, st,
    lam_next, zl_next, u_next, rim, rim_next,
    acc, stage_lo, stage_hi, recv_lo, recv_hi,
    part, part_tm, part_sp,
    load_sem, slo_sem, shi_sem, rlo_sem, rhi_sem, tms_sem, tmr_sem,
    ptm_s, ptm_r, psp_s, psp_r, out_sem,
):
    steps, lev, rows, nlon = ro.shape
    last = rows - 1
    tm = lax.axis_index("tm")
    sp = lax.axis_index("space")
    has_lo, has_hi = sp > 0, sp < nsp - 1
    has_prev, has_next = tm > 0, tm < ntm - 1

    loads = {}

    def load(name, src, dst):
        copy = pltpu.make_async_copy(src, dst, load_sem.at[len(loads)])
        copy.start()
        loads[name] = copy

    load("rs", rs_h, rs)
    load("mv", mv_h, mv)
    for j in reversed(range(steps)):
        load(("mk", j), mk_h.at[j], mk.at[j])
        load(("ro", j), ro_h.at[j], ro.at[j])
        load(("wn", j), wn_h.at[j], wn.at[j])
        load(("we", j), we_h.at[j], we.at[j])
    for j in reversed(range(steps)):
        load(("ov", j), ov_h.at[j], ov.at[j])

    barrier = pltpu.get_barrier_semaphore()
    for d in range(1, ntm):
        pl.semaphore_signal(barrier, inc=1, device_id=(lax.rem(tm + d, ntm), sp), device_id_type=MESH)
    for d in range(1, nsp):
        pl.semaphore_signal(barrier, inc=1, device_id=(tm, lax.rem(sp + d, nsp)), device_id_type=MESH)
    pl.semaphore_wait(barrier, ntm + nsp - 2)

    def tm_copy(i, src, dst, device):
        return pltpu.make_async_remote_copy(
            src_ref=src, dst_ref=dst, send_sem=tms_sem.at[i], recv_sem=tmr_sem.at[i],
            device_id=(device, sp), device_id_type=MESH,
        )

    def tm_send(i, src, dst):
        @pl.when(has_prev)
        def _():
            tm_copy(i, src, dst, tm - 1).start()

    def tm_recv(i, src, dst):
        @pl.when(has_next)
        def _():
            tm_copy(i, src, dst, tm + 1).wait_recv()

    def to_lo(slot, device):
        return pltpu.make_async_remote_copy(
            src_ref=stage_lo.at[slot], dst_ref=recv_hi.at[slot],
            send_sem=slo_sem.at[slot], recv_sem=rhi_sem.at[slot],
            device_id=(tm, device), device_id_type=MESH,
        )

    def to_hi(slot, device):
        return pltpu.make_async_remote_copy(
            src_ref=stage_hi.at[slot], dst_ref=recv_lo.at[slot],
            send_sem=shi_sem.at[slot], recv_sem=rlo_sem.at[slot],
            device_id=(tm, device), device_id_type=MESH,
        )

    row = lax.broadcasted_iota(jnp.int32, (rows, nlon), 0)

    def down(x):
        return jnp.where(row == 0, 0.0, pltpu.roll(x, 1, 0))

    def up(x):
        return jnp.where(row == last, 0.0, pltpu.roll(x, rows - 1, 0))

    def before(x):
        return pltpu.roll(x, 1, 1)

    def after(x):
        return pltpu.roll(x, nlon - 1, 1)

    def fold(x):
        total = x[0:8]
        for i in range(8, rows, 8):
            total = total + x[i:i + 8]
        return total

    def levels(body):
        lax.fori_loop(0, lev, lambda l, c: (body(l), c)[1], 0)

    loads["rs"].wait()
    for l in range(lev):
        rim[0, l:l + 1, :] = rs[l, 0:1, :]
        rim[1, l:l + 1, :] = rs[l, last:rows, :]
    tm_send(3, rim, rim_next)
    tm_send(0, rs, lam_next)
    loads["mv"].wait()

    def _(l):
        z = mv[l] * rs[l]
        zl[l] = z
        acc[0, l] = fold(z * rs[l])
        acc[1, l] = fold(z * z)
        acc[2, l] = jnp.zeros((8, nlon), jnp.float32)
        acc[3, l] = jnp.zeros((8, nlon), jnp.float32)
    levels(_)
    tm_send(1, zl, zl_next)

    @pl.when(jnp.logical_not(has_next))
    def _():
        rim_next[...] = jnp.zeros_like(rim_next)
        lam_next[...] = jnp.zeros_like(lam_next)
        zl_next[...] = jnp.zeros_like(zl_next)

    def mask(j, l):
        return mk[j, l].astype(jnp.float32)

    for name in ("mk", "ro", "wn", "we"):
        loads[name, steps - 1].wait()
    def first_row(side, i, l):
        j = steps - 1
        seen = mk[j, l, i:i + 1, :].astype(jnp.float32)
        return seen * ro[j, l, i:i + 1, :] - rim_next[side, l:l + 1, :]

    def send_adjoint(slot, t, j):
        def _(l):
            if slot == 0:
                lo, hi = first_row(0, 0, l), first_row(1, last, l)
            else:
                lo, hi = t[l, 0:1, :], t[l, last:rows, :]
            stage_lo[slot, pl.ds(l, 1), :] = KAPPA * lo + 0.5 * (wn[j, l, 0:1, :] * lo)
            stage_hi[slot, pl.ds(l, 1), :] = KAPPA * hi - 0.5 * (wn[j, l, last:rows, :] * hi)
        for l in range(lev):
            _(l)
        start(slot)

    def send_forward(slot, s):
        for l in range(lev):
            stage_lo[slot, pl.ds(l, 1), :] = s[l, 0:1, :]
            stage_hi[slot, pl.ds(l, 1), :] = s[l, last:rows, :]
        start(slot)

    def start(slot):
        @pl.when(has_lo)
        def _():
            to_lo(slot, sp - 1).start()

        @pl.when(has_hi)
        def _():
            to_hi(slot, sp + 1).start()

    def finish(slot, t, j=None):
        @pl.when(has_lo)
        def _():
            to_hi(slot, sp - 1).wait_recv()
            for l in range(lev):
                got = recv_lo[slot, pl.ds(l, 1), :]
                if j is not None:
                    got = (KAPPA + 0.5 * wn[j, l, 0:1, :]) * got
                t[l, 0:1, :] = t[l, 0:1, :] + got

        @pl.when(has_hi)
        def _():
            to_lo(slot, sp + 1).wait_recv()
            for l in range(lev):
                got = recv_hi[slot, pl.ds(l, 1), :]
                if j is not None:
                    got = (KAPPA - 0.5 * wn[j, l, last:rows, :]) * got
                t[l, last:rows, :] = t[l, last:rows, :] + got

    def transposed(t, j, l):
        x = t[l]
        k = KAPPA * x
        e = 0.5 * (we[j, l] * x)
        n = 0.5 * (wn[j, l] * x)
        return (1.0 - 4.0 * KAPPA) * x + before(k - e) + after(k + e) + down(k - n) + up(k + n)

    def adjoint1(j):
        if j > 0:
            def _(l):
                t1[l] = transposed(t1, j, l) + mask(j - 1, l) * ro[j - 1, l]
        else:
            def _(l):
                zdx[l] = transposed(t1, j, l) + rs[l]
        levels(_)

    def inject2(j, l):
        z = ov[j, l] * ro[j, l]
        acc[0, l] += fold(z * ro[j, l])
        acc[1, l] += fold(z * z)
        return mask(j, l) * z

    def adjoint2(j):
        if j > 0:
            def _(l):
                t2[l] = transposed(t2, j, l) + inject2(j - 1, l)
        else:
            def _(l):
                t2[l] = transposed(t2, j, l) + zl[l]
        levels(_)

    def observed(j, l, s):
        z = ov[j, l] * ro[j, l]
        w = ov[j, l] * z + mask(j, l) * s
        acc[2, l] += fold(z * w)
        acc[3, l] += fold(w * w)

    def forward(src, j):
        def _(l):
            x = src[l]
            if j > 0:
                observed(j - 1, l, x)
            else:
                acc[1, l] += fold(x * x)
                u[l] = mv[l] * zl[l] + x
            e, w = after(x), before(x)
            n, s = up(x), down(x)
            st[l] = (
                x
                - 0.5 * (we[j, l] * (e - w))
                - 0.5 * (wn[j, l] * (n - s))
                + KAPPA * (e + w + n + s - 4.0 * x)
            )
        levels(_)

    def start2():
        for j in reversed(range(steps)):
            loads["ov", j].wait()
        tm_recv(1, zl, zl_next)

        def _(l):
            t2[l] = inject2(steps - 1, l) - zl_next[l]
        levels(_)

    def round2(q):
        j = steps - 1 - q
        if q == 0:
            start2()
        else:
            finish(2 * steps + q - 1, t2)
        if q < steps:
            send_adjoint(2 * steps + q, t2, j)
            adjoint2(j)

    def own_window():
        @pl.when(jnp.logical_not(has_prev))
        def _():
            def _(l):
                acc[2, l] += fold(zl[l] * u[l])
                acc[3, l] += fold(u[l] * u[l])
            levels(_)

    def increments():
        def _(l):
            acc[2, l] += fold(zdx[l] * t2[l])
            acc[3, l] += fold(t2[l] * t2[l])
        levels(_)

    lag = steps // 2
    for r in range(2 * steps):
        if r < steps:
            j = steps - 1 - r
            if r == 0:
                tm_recv(3, rim, rim_next)
            send_adjoint(r, t1, j)
            if r == 0:
                tm_recv(0, rs, lam_next)

                def _(l):
                    t1[l] = mask(steps - 1, l) * ro[steps - 1, l] - lam_next[l]
                levels(_)
            if j > 0:
                for name in ("mk", "ro", "wn", "we"):
                    loads[name, j - 1].wait()
            adjoint1(j)
            target = t1 if j > 0 else zdx
            weight = None
        else:
            j = r - steps
            src = zdx if j == 0 else st
            send_forward(r, src)
            if j == 0:
                out = pltpu.make_async_copy(zdx, zdx_h, out_sem)
                out.start()
            forward(src, j)
            if j == 0:
                tm_send(2, u, u_next)
            target, weight = st, j
        if lag <= r <= lag + steps:
            round2(r - lag)
        if r == lag + steps:
            increments()
        if r == 2 * steps - 1:
            own_window()
            tm_recv(2, u, u_next)
        finish(r, target, weight)

    def _(l):
        observed(steps - 1, l, st[l])
    levels(_)

    @pl.when(has_next)
    def _():
        def _(l):
            w = u_next[l] - st[l]
            acc[2, l] += fold(zl_next[l] * w)
            acc[3, l] += fold(w * w)
        levels(_)

    for i in range(4):
        total = acc[i, 0]
        for l in range(1, lev):
            total = total + acc[i, l]
        lanes = total[:, 0:128]
        for c in range(128, nlon, 128):
            lanes = lanes + total[:, c:c + 128]
        part[0, i:i + 1, :] = jnp.sum(lanes, axis=0, keepdims=True)
    part[0, 4:8, :] = jnp.zeros((4, 128), jnp.float32)

    def gather(count, slots, sends, recvs, device, src):
        copies = [
            pltpu.make_async_remote_copy(
                src_ref=src, dst_ref=slots.at[d - 1],
                send_sem=sends.at[d - 1], recv_sem=recvs.at[d - 1],
                device_id=device(d), device_id_type=MESH,
            )
            for d in range(1, count)
        ]
        for copy in copies:
            copy.start()
        total = src[...]
        for d, copy in enumerate(copies):
            copy.wait_recv()
            total = total + slots[d]
        return total, copies

    total, copies1 = gather(
        ntm, part_tm, ptm_s, ptm_r, lambda d: (lax.rem(tm + d, ntm), sp), part.at[0]
    )
    part[1] = total
    total, copies2 = gather(
        nsp, part_sp, psp_s, psp_r, lambda d: (tm, lax.rem(sp + d, nsp)), part.at[1]
    )
    sums = jnp.broadcast_to(jnp.sum(total, axis=1, keepdims=True), (8, 128))
    n, d, e, f = (sums[i:i + 1, :] for i in range(4))
    first = n / d
    second = first * (first * e - d) / (d - 2.0 * first * e + first * first * f)
    coef_ref[0:1, :] = first + second
    coef_ref[1:2, :] = -(first * second)
    coef_ref[2:8, :] = jnp.zeros((6, 128), jnp.float32)

    for copy in copies1 + copies2:
        copy.wait_send()
    for slot in range(3 * steps):
        @pl.when(has_lo)
        def _(slot=slot):
            to_lo(slot, sp - 1).wait_send()

        @pl.when(has_hi)
        def _(slot=slot):
            to_hi(slot, sp + 1).wait_send()

    @pl.when(has_prev)
    def _():
        tm_copy(3, rim, rim_next, tm - 1).wait_send()
        tm_copy(0, rs, lam_next, tm - 1).wait_send()
        tm_copy(1, zl, zl_next, tm - 1).wait_send()
        tm_copy(2, u, u_next, tm - 1).wait_send()
    out.wait()


def combine(coef_h, zdx_h, rs, ro, mv, ov, lam_h, mu_h, dx_h, lam, mu, dx, coef, zdx, sem, in_sem):
    get_coef = pltpu.make_async_copy(coef_h, coef, in_sem.at[0])
    get_zdx = pltpu.make_async_copy(zdx_h, zdx, in_sem.at[1])
    get_coef.start()
    get_zdx.start()
    get_coef.wait()
    steps, lev, rows, nlon = ro.shape
    both = jnp.broadcast_to(coef[0:1, 0:1], (rows, nlon))
    cross = jnp.broadcast_to(coef[1:2, 0:1], (rows, nlon))
    copies = []

    def put(body, src, dst):
        lax.fori_loop(0, lev, lambda l, c: (body(l), c)[1], 0)
        copy = pltpu.make_async_copy(src, dst, sem.at[len(copies)])
        copy.start()
        copies.append(copy)

    for j in range(steps):
        def _(l, j=j):
            mu[j, l] = (both + cross * ov[j, l]) * ro[j, l]
        put(_, mu.at[j], mu_h.at[j])

    def _(l):
        lam[l] = (both + cross * mv[l]) * rs[l]
    put(_, lam, lam_h)

    get_zdx.wait()

    def _(l):
        dx[l] = cross * zdx[l]
    put(_, dx, dx_h)
    for copy in copies:
        copy.wait()


def on_device(ntm, nsp, *args):
    rhs_state, rhs_obs, wind_east, wind_north, model_var, obs_var, obs_mask = (a[0] for a in args)
    steps, lev, rows, nlon = rhs_obs.shape
    f32 = jnp.float32
    field = pltpu.VMEM((lev, rows, nlon), f32)
    fields = pltpu.VMEM((steps, lev, rows, nlon), f32)
    slots = 3 * steps
    halo = pltpu.VMEM((slots, lev, nlon), f32)
    rim = pltpu.VMEM((2, lev, nlon), f32)
    dma = pltpu.SemaphoreType.DMA
    hbm = pl.BlockSpec(memory_space=pl.ANY)
    zdx, coef = pl.pallas_call(
        functools.partial(kernel, ntm, nsp),
        out_shape=(
            jax.ShapeDtypeStruct((lev, rows, nlon), f32),
            jax.ShapeDtypeStruct((8, 128), f32),
        ),
        in_specs=[hbm] * 7,
        out_specs=(hbm, pl.BlockSpec(memory_space=pltpu.VMEM)),
        scratch_shapes=[
            field, fields, fields, fields, field, fields,
            pltpu.VMEM((steps, lev, rows, nlon), jnp.int32),
            field, field, field, field, field, field,
            field, field, field, rim, rim,
            pltpu.VMEM((4, lev, 8, nlon), f32), halo, halo, halo, halo,
            pltpu.VMEM((2, 8, 128), f32),
            pltpu.VMEM((ntm - 1, 8, 128), f32),
            pltpu.VMEM((nsp - 1, 8, 128), f32),
            dma((2 + 5 * steps,)), dma((slots,)), dma((slots,)), dma((slots,)), dma((slots,)),
            dma((4,)), dma((4,)),
            dma((ntm - 1,)), dma((ntm - 1,)), dma((nsp - 1,)), dma((nsp - 1,)), dma,
        ],
        compiler_params=pltpu.CompilerParams(
            collective_id=0, has_side_effects=True, vmem_limit_bytes=56 * 1024 * 1024
        ),
    )(rhs_state, rhs_obs, wind_east, wind_north, model_var, obs_var, obs_mask)
    vmem = pl.BlockSpec(memory_space=pltpu.VMEM)
    lam, mu, dx = pl.pallas_call(
        combine,
        out_shape=(
            jax.ShapeDtypeStruct((lev, rows, nlon), f32),
            jax.ShapeDtypeStruct((steps, lev, rows, nlon), f32),
            jax.ShapeDtypeStruct((lev, rows, nlon), f32),
        ),
        in_specs=[hbm] * 2 + [vmem] * 4,
        out_specs=(hbm, hbm, hbm),
        scratch_shapes=[
            field, fields, field, pltpu.VMEM((8, 128), f32), field, dma((steps + 2,)), dma((2,)),
        ],
        compiler_params=pltpu.CompilerParams(vmem_limit_bytes=16 * 1024 * 1024),
    )(coef, zdx, rhs_state, rhs_obs, model_var, obs_var)
    return lam[None], mu[None], dx[None]


def solution(mesh):
    flat = P("tm", None, "space", None)
    deep = P("tm", None, None, "space", None)
    return jax.shard_map(
        functools.partial(on_device, mesh.shape["tm"], mesh.shape["space"]),
        mesh=mesh,
        in_specs=(flat, deep, deep, deep, flat, deep, deep),
        out_specs=(flat, deep, flat),
        check_vma=False,
    )
```

```python
import functools

import jax
import jax.numpy as jnp
from jax import lax
from jax.experimental import pallas as pl
from jax.experimental.pallas import tpu as pltpu
from jax.sharding import PartitionSpec as P

KAPPA = 0.12
MESH = pl.DeviceIdType.MESH


def kernel(
    ntm, nsp,
    rs_h, ro_h, we_h, wn_h, mv_h, ov_h, mk_h,
    zdx_h, coef_ref,
    rs, ro, we, wn, mv, ov, mk,
    zl, zdx, u, t1, t2, st,
    lam_next, zl_next, u_next, rim, rim_next,
    acc, stage_lo, stage_hi, recv_lo, recv_hi,
    part, part_tm, part_sp,
    load_sem, slo_sem, shi_sem, rlo_sem, rhi_sem, tms_sem, tmr_sem,
    ptm_s, ptm_r, psp_s, psp_r, out_sem,
):
    steps, lev, rows, nlon = ro.shape
    last = rows - 1
    tm = lax.axis_index("tm")
    sp = lax.axis_index("space")
    has_lo, has_hi = sp > 0, sp < nsp - 1
    has_prev, has_next = tm > 0, tm < ntm - 1

    loads = {}

    def load(name, src, dst):
        copy = pltpu.make_async_copy(src, dst, load_sem.at[len(loads)])
        copy.start()
        loads[name] = copy

    load("rs", rs_h, rs)
    load("mv", mv_h, mv)
    for j in reversed(range(steps)):
        load(("mk", j), mk_h.at[j], mk.at[j])
        load(("ro", j), ro_h.at[j], ro.at[j])
        load(("wn", j), wn_h.at[j], wn.at[j])
        load(("we", j), we_h.at[j], we.at[j])
    for j in reversed(range(steps)):
        load(("ov", j), ov_h.at[j], ov.at[j])

    barrier = pltpu.get_barrier_semaphore()
    for d in range(1, ntm):
        pl.semaphore_signal(barrier, inc=1, device_id=(lax.rem(tm + d, ntm), sp), device_id_type=MESH)
    for d in range(1, nsp):
        pl.semaphore_signal(barrier, inc=1, device_id=(tm, lax.rem(sp + d, nsp)), device_id_type=MESH)
    pl.semaphore_wait(barrier, ntm + nsp - 2)

    def tm_copy(i, src, dst, device):
        return pltpu.make_async_remote_copy(
            src_ref=src, dst_ref=dst, send_sem=tms_sem.at[i], recv_sem=tmr_sem.at[i],
            device_id=(device, sp), device_id_type=MESH,
        )

    def tm_send(i, src, dst):
        @pl.when(has_prev)
        def _():
            tm_copy(i, src, dst, tm - 1).start()

    def tm_recv(i, src, dst):
        @pl.when(has_next)
        def _():
            tm_copy(i, src, dst, tm + 1).wait_recv()

    def to_lo(slot, device):
        return pltpu.make_async_remote_copy(
            src_ref=stage_lo.at[slot], dst_ref=recv_hi.at[slot],
            send_sem=slo_sem.at[slot], recv_sem=rhi_sem.at[slot],
            device_id=(tm, device), device_id_type=MESH,
        )

    def to_hi(slot, device):
        return pltpu.make_async_remote_copy(
            src_ref=stage_hi.at[slot], dst_ref=recv_lo.at[slot],
            send_sem=shi_sem.at[slot], recv_sem=rlo_sem.at[slot],
            device_id=(tm, device), device_id_type=MESH,
        )

    row = lax.broadcasted_iota(jnp.int32, (rows, nlon), 0)

    def down(x):
        return jnp.where(row == 0, 0.0, pltpu.roll(x, 1, 0))

    def up(x):
        return jnp.where(row == last, 0.0, pltpu.roll(x, rows - 1, 0))

    def before(x):
        return pltpu.roll(x, 1, 1)

    def after(x):
        return pltpu.roll(x, nlon - 1, 1)

    def fold(x):
        total = x[0:8]
        for i in range(8, rows, 8):
            total = total + x[i:i + 8]
        return total

    def levels(body):
        lax.fori_loop(0, lev, lambda l, c: (body(l), c)[1], 0)

    loads["rs"].wait()
    for l in range(lev):
        rim[0, l:l + 1, :] = rs[l, 0:1, :]
        rim[1, l:l + 1, :] = rs[l, last:rows, :]
    tm_send(3, rim, rim_next)
    for l in range(lev):
        tm_send(4 + l, rs.at[l], lam_next.at[l])
    loads["mv"].wait()

    def _(l):
        z = mv[l] * rs[l]
        zl[l] = z
        acc[0, l] = fold(z * rs[l])
        acc[1, l] = fold(z * z)
        acc[2, l] = jnp.zeros((8, nlon), jnp.float32)
        acc[3, l] = jnp.zeros((8, nlon), jnp.float32)
    levels(_)
    tm_send(1, zl, zl_next)

    @pl.when(jnp.logical_not(has_next))
    def _():
        rim_next[...] = jnp.zeros_like(rim_next)
        lam_next[...] = jnp.zeros_like(lam_next)
        zl_next[...] = jnp.zeros_like(zl_next)

    def mask(j, l):
        return mk[j, l].astype(jnp.float32)

    for name in ("mk", "ro", "wn", "we"):
        loads[name, steps - 1].wait()
    def first_row(side, i, l):
        j = steps - 1
        seen = mk[j, l, i:i + 1, :].astype(jnp.float32)
        return seen * ro[j, l, i:i + 1, :] - rim_next[side, l:l + 1, :]

    def send_adjoint(slot, t, j):
        def _(l):
            if slot == 0:
                lo, hi = first_row(0, 0, l), first_row(1, last, l)
            else:
                lo, hi = t[l, 0:1, :], t[l, last:rows, :]
            stage_lo[slot, pl.ds(l, 1), :] = KAPPA * lo + 0.5 * (wn[j, l, 0:1, :] * lo)
            stage_hi[slot, pl.ds(l, 1), :] = KAPPA * hi - 0.5 * (wn[j, l, last:rows, :] * hi)
        for l in range(lev):
            _(l)
        start(slot)

    def send_forward(slot, s):
        for l in range(lev):
            stage_lo[slot, pl.ds(l, 1), :] = s[l, 0:1, :]
            stage_hi[slot, pl.ds(l, 1), :] = s[l, last:rows, :]
        start(slot)

    def start(slot):
        @pl.when(has_lo)
        def _():
            to_lo(slot, sp - 1).start()

        @pl.when(has_hi)
        def _():
            to_hi(slot, sp + 1).start()

    def finish(slot, t, j=None):
        @pl.when(has_lo)
        def _():
            to_hi(slot, sp - 1).wait_recv()
            for l in range(lev):
                got = recv_lo[slot, pl.ds(l, 1), :]
                if j is not None:
                    got = (KAPPA + 0.5 * wn[j, l, 0:1, :]) * got
                t[l, 0:1, :] = t[l, 0:1, :] + got

        @pl.when(has_hi)
        def _():
            to_lo(slot, sp + 1).wait_recv()
            for l in range(lev):
                got = recv_hi[slot, pl.ds(l, 1), :]
                if j is not None:
                    got = (KAPPA - 0.5 * wn[j, l, last:rows, :]) * got
                t[l, last:rows, :] = t[l, last:rows, :] + got

    def transposed(t, j, l):
        x = t[l]
        k = KAPPA * x
        e = 0.5 * (we[j, l] * x)
        n = 0.5 * (wn[j, l] * x)
        return (1.0 - 4.0 * KAPPA) * x + before(k - e) + after(k + e) + down(k - n) + up(k + n)

    def adjoint1(j):
        if j > 0:
            def _(l):
                if j == steps - 1:
                    tm_recv(4 + l, rs.at[l], lam_next.at[l])
                    t1[l] = mask(j, l) * ro[j, l] - lam_next[l]
                t1[l] = transposed(t1, j, l) + mask(j - 1, l) * ro[j - 1, l]
        else:
            def _(l):
                zdx[l] = transposed(t1, j, l) + rs[l]
        levels(_)

    def inject2(j, l):
        z = ov[j, l] * ro[j, l]
        acc[0, l] += fold(z * ro[j, l])
        acc[1, l] += fold(z * z)
        return mask(j, l) * z

    def adjoint2(j):
        if j > 0:
            def _(l):
                t2[l] = transposed(t2, j, l) + inject2(j - 1, l)
        else:
            def _(l):
                t2[l] = transposed(t2, j, l) + zl[l]
        levels(_)

    def observed(j, l, s):
        z = ov[j, l] * ro[j, l]
        w = ov[j, l] * z + mask(j, l) * s
        acc[2, l] += fold(z * w)
        acc[3, l] += fold(w * w)

    def forward(src, j):
        def _(l):
            x = src[l]
            if j > 0:
                observed(j - 1, l, x)
            else:
                acc[1, l] += fold(x * x)
                u[l] = mv[l] * zl[l] + x
            e, w = after(x), before(x)
            n, s = up(x), down(x)
            st[l] = (
                x
                - 0.5 * (we[j, l] * (e - w))
                - 0.5 * (wn[j, l] * (n - s))
                + KAPPA * (e + w + n + s - 4.0 * x)
            )
        levels(_)

    def start2():
        for j in reversed(range(steps)):
            loads["ov", j].wait()
        tm_recv(1, zl, zl_next)

        def _(l):
            t2[l] = inject2(steps - 1, l) - zl_next[l]
        levels(_)

    def round2(q):
        j = steps - 1 - q
        if q == 0:
            start2()
        else:
            finish(2 * steps + q - 1, t2)
        if q < steps:
            send_adjoint(2 * steps + q, t2, j)
            adjoint2(j)

    def own_window():
        @pl.when(jnp.logical_not(has_prev))
        def _():
            def _(l):
                acc[2, l] += fold(zl[l] * u[l])
                acc[3, l] += fold(u[l] * u[l])
            levels(_)

    def increments():
        def _(l):
            acc[2, l] += fold(zdx[l] * t2[l])
            acc[3, l] += fold(t2[l] * t2[l])
        levels(_)

    lag = steps // 2
    for r in range(2 * steps):
        if r < steps:
            j = steps - 1 - r
            if r == 0:
                tm_recv(3, rim, rim_next)
            send_adjoint(r, t1, j)
            if j > 0:
                for name in ("mk", "ro", "wn", "we"):
                    loads[name, j - 1].wait()
            adjoint1(j)
            target = t1 if j > 0 else zdx
            weight = None
        else:
            j = r - steps
            src = zdx if j == 0 else st
            send_forward(r, src)
            if j == 0:
                out = pltpu.make_async_copy(zdx, zdx_h, out_sem)
                out.start()
            forward(src, j)
            if j == 0:
                tm_send(2, u, u_next)
            target, weight = st, j
        if lag <= r <= lag + steps:
            round2(r - lag)
        if r == lag + steps:
            increments()
        if r == 2 * steps - 1:
            own_window()
            tm_recv(2, u, u_next)
        finish(r, target, weight)

    def _(l):
        observed(steps - 1, l, st[l])
    levels(_)

    @pl.when(has_next)
    def _():
        def _(l):
            w = u_next[l] - st[l]
            acc[2, l] += fold(zl_next[l] * w)
            acc[3, l] += fold(w * w)
        levels(_)

    for i in range(4):
        total = acc[i, 0]
        for l in range(1, lev):
            total = total + acc[i, l]
        lanes = total[:, 0:128]
        for c in range(128, nlon, 128):
            lanes = lanes + total[:, c:c + 128]
        part[0, i:i + 1, :] = jnp.sum(lanes, axis=0, keepdims=True)
    part[0, 4:8, :] = jnp.zeros((4, 128), jnp.float32)

    def gather(count, slots, sends, recvs, device, src):
        copies = [
            pltpu.make_async_remote_copy(
                src_ref=src, dst_ref=slots.at[d - 1],
                send_sem=sends.at[d - 1], recv_sem=recvs.at[d - 1],
                device_id=device(d), device_id_type=MESH,
            )
            for d in range(1, count)
        ]
        for copy in copies:
            copy.start()
        total = src[...]
        for d, copy in enumerate(copies):
            copy.wait_recv()
            total = total + slots[d]
        return total, copies

    total, copies1 = gather(
        ntm, part_tm, ptm_s, ptm_r, lambda d: (lax.rem(tm + d, ntm), sp), part.at[0]
    )
    part[1] = total
    total, copies2 = gather(
        nsp, part_sp, psp_s, psp_r, lambda d: (tm, lax.rem(sp + d, nsp)), part.at[1]
    )
    sums = jnp.broadcast_to(jnp.sum(total, axis=1, keepdims=True), (8, 128))
    n, d, e, f = (sums[i:i + 1, :] for i in range(4))
    first = n / d
    second = first * (first * e - d) / (d - 2.0 * first * e + first * first * f)
    coef_ref[0:1, :] = first + second
    coef_ref[1:2, :] = -(first * second)
    coef_ref[2:8, :] = jnp.zeros((6, 128), jnp.float32)

    for copy in copies1 + copies2:
        copy.wait_send()
    for slot in range(3 * steps):
        @pl.when(has_lo)
        def _(slot=slot):
            to_lo(slot, sp - 1).wait_send()

        @pl.when(has_hi)
        def _(slot=slot):
            to_hi(slot, sp + 1).wait_send()

    @pl.when(has_prev)
    def _():
        tm_copy(3, rim, rim_next, tm - 1).wait_send()
        for l in range(lev):
            tm_copy(4 + l, rs.at[l], lam_next.at[l], tm - 1).wait_send()
        tm_copy(1, zl, zl_next, tm - 1).wait_send()
        tm_copy(2, u, u_next, tm - 1).wait_send()
    out.wait()


def combine(coef_h, zdx_h, rs, ro, mv, ov, lam_h, mu_h, dx_h, lam, mu, dx, coef, zdx, sem, in_sem):
    get_coef = pltpu.make_async_copy(coef_h, coef, in_sem.at[0])
    get_zdx = pltpu.make_async_copy(zdx_h, zdx, in_sem.at[1])
    get_coef.start()
    get_zdx.start()
    get_coef.wait()
    steps, lev, rows, nlon = ro.shape
    both = jnp.broadcast_to(coef[0:1, 0:1], (rows, nlon))
    cross = jnp.broadcast_to(coef[1:2, 0:1], (rows, nlon))
    copies = []

    def put(body, src, dst):
        lax.fori_loop(0, lev, lambda l, c: (body(l), c)[1], 0)
        copy = pltpu.make_async_copy(src, dst, sem.at[len(copies)])
        copy.start()
        copies.append(copy)

    for j in range(steps):
        def _(l, j=j):
            mu[j, l] = (both + cross * ov[j, l]) * ro[j, l]
        put(_, mu.at[j], mu_h.at[j])

    def _(l):
        lam[l] = (both + cross * mv[l]) * rs[l]
    put(_, lam, lam_h)

    get_zdx.wait()

    def _(l):
        dx[l] = cross * zdx[l]
    put(_, dx, dx_h)
    for copy in copies:
        copy.wait()


def on_device(ntm, nsp, *args):
    rhs_state, rhs_obs, wind_east, wind_north, model_var, obs_var, obs_mask = (a[0] for a in args)
    steps, lev, rows, nlon = rhs_obs.shape
    f32 = jnp.float32
    field = pltpu.VMEM((lev, rows, nlon), f32)
    fields = pltpu.VMEM((steps, lev, rows, nlon), f32)
    slots = 3 * steps
    halo = pltpu.VMEM((slots, lev, nlon), f32)
    rim = pltpu.VMEM((2, lev, nlon), f32)
    dma = pltpu.SemaphoreType.DMA
    hbm = pl.BlockSpec(memory_space=pl.ANY)
    zdx, coef = pl.pallas_call(
        functools.partial(kernel, ntm, nsp),
        out_shape=(
            jax.ShapeDtypeStruct((lev, rows, nlon), f32),
            jax.ShapeDtypeStruct((8, 128), f32),
        ),
        in_specs=[hbm] * 7,
        out_specs=(hbm, pl.BlockSpec(memory_space=pltpu.VMEM)),
        scratch_shapes=[
            field, fields, fields, fields, field, fields,
            pltpu.VMEM((steps, lev, rows, nlon), jnp.int32),
            field, field, field, field, field, field,
            field, field, field, rim, rim,
            pltpu.VMEM((4, lev, 8, nlon), f32), halo, halo, halo, halo,
            pltpu.VMEM((2, 8, 128), f32),
            pltpu.VMEM((ntm - 1, 8, 128), f32),
            pltpu.VMEM((nsp - 1, 8, 128), f32),
            dma((2 + 5 * steps,)), dma((slots,)), dma((slots,)), dma((slots,)), dma((slots,)),
            dma((4 + lev,)), dma((4 + lev,)),
            dma((ntm - 1,)), dma((ntm - 1,)), dma((nsp - 1,)), dma((nsp - 1,)), dma,
        ],
        compiler_params=pltpu.CompilerParams(
            collective_id=0, has_side_effects=True, vmem_limit_bytes=54656 * 1024
        ),
    )(rhs_state, rhs_obs, wind_east, wind_north, model_var, obs_var, obs_mask)
    vmem = pl.BlockSpec(memory_space=pltpu.VMEM)
    lam, mu, dx = pl.pallas_call(
        combine,
        out_shape=(
            jax.ShapeDtypeStruct((lev, rows, nlon), f32),
            jax.ShapeDtypeStruct((steps, lev, rows, nlon), f32),
            jax.ShapeDtypeStruct((lev, rows, nlon), f32),
        ),
        in_specs=[hbm] * 2 + [vmem] * 4,
        out_specs=(hbm, hbm, hbm),
        scratch_shapes=[
            field, fields, field, pltpu.VMEM((8, 128), f32), field, dma((steps + 2,)), dma((2,)),
        ],
        compiler_params=pltpu.CompilerParams(vmem_limit_bytes=16 * 1024 * 1024),
    )(coef, zdx, rhs_state, rhs_obs, model_var, obs_var)
    return lam[None], mu[None], dx[None]


def solution(mesh):
    flat = P("tm", None, "space", None)
    deep = P("tm", None, None, "space", None)
    return jax.shard_map(
        functools.partial(on_device, mesh.shape["tm"], mesh.shape["space"]),
        mesh=mesh,
        in_specs=(flat, deep, deep, deep, flat, deep, deep),
        out_specs=(flat, deep, flat),
        check_vma=False,
    )
```

```python
import functools

import jax
import jax.numpy as jnp
from jax import lax
from jax.experimental import pallas as pl
from jax.experimental.pallas import tpu as pltpu
from jax.sharding import PartitionSpec as P

KAPPA = 0.12
MESH = pl.DeviceIdType.MESH


def kernel(
    ntm, nsp,
    rs_h, ro_h, we_h, wn_h, mv_h, ov_h, mk_h,
    zdx_h, coef_ref,
    rs, ro, we, wn, mv, ov, mk,
    zl, zdx, u, t1, t2, st,
    lam_next, zl_next, u_next, rim, rim_next,
    acc, stage_lo, stage_hi, recv_lo, recv_hi,
    part, part_tm, part_sp,
    load_sem, slo_sem, shi_sem, rlo_sem, rhi_sem, tms_sem, tmr_sem,
    ptm_s, ptm_r, psp_s, psp_r, out_sem,
):
    steps, lev, rows, nlon = ro.shape
    last = rows - 1
    tm = lax.axis_index("tm")
    sp = lax.axis_index("space")
    has_lo, has_hi = sp > 0, sp < nsp - 1
    has_prev, has_next = tm > 0, tm < ntm - 1

    loads = {}

    def load(name, src, dst):
        copy = pltpu.make_async_copy(src, dst, load_sem.at[len(loads)])
        copy.start()
        loads[name] = copy

    load("rs", rs_h, rs)
    load("mv", mv_h, mv)
    for j in reversed(range(steps)):
        load(("mk", j), mk_h.at[j], mk.at[j])
        load(("ro", j), ro_h.at[j], ro.at[j])
        load(("wn", j), wn_h.at[j], wn.at[j])
        load(("we", j), we_h.at[j], we.at[j])
    for j in reversed(range(steps)):
        load(("ov", j), ov_h.at[j], ov.at[j])

    barrier = pltpu.get_barrier_semaphore()
    total_devices = ntm * nsp
    flat = total_devices <= 64

    def any_device(d):
        at = lax.rem(tm * nsp + sp + d, total_devices)
        return (lax.div(at, nsp), lax.rem(at, nsp))

    if flat:
        peers = [any_device(d) for d in range(1, total_devices)]
    else:
        peers = [(lax.rem(tm + d, ntm), sp) for d in range(1, ntm)]
        peers += [(tm, lax.rem(sp + d, nsp)) for d in range(1, nsp)]
    for peer in peers:
        pl.semaphore_signal(barrier, inc=1, device_id=peer, device_id_type=MESH)
    pl.semaphore_wait(barrier, len(peers))

    def tm_copy(i, src, dst, device):
        return pltpu.make_async_remote_copy(
            src_ref=src, dst_ref=dst, send_sem=tms_sem.at[i], recv_sem=tmr_sem.at[i],
            device_id=(device, sp), device_id_type=MESH,
        )

    def tm_send(i, src, dst):
        @pl.when(has_prev)
        def _():
            tm_copy(i, src, dst, tm - 1).start()

    def tm_recv(i, src, dst):
        @pl.when(has_next)
        def _():
            tm_copy(i, src, dst, tm + 1).wait_recv()

    def to_lo(slot, device):
        return pltpu.make_async_remote_copy(
            src_ref=stage_lo.at[slot], dst_ref=recv_hi.at[slot],
            send_sem=slo_sem.at[slot], recv_sem=rhi_sem.at[slot],
            device_id=(tm, device), device_id_type=MESH,
        )

    def to_hi(slot, device):
        return pltpu.make_async_remote_copy(
            src_ref=stage_hi.at[slot], dst_ref=recv_lo.at[slot],
            send_sem=shi_sem.at[slot], recv_sem=rlo_sem.at[slot],
            device_id=(tm, device), device_id_type=MESH,
        )

    row = lax.broadcasted_iota(jnp.int32, (rows, nlon), 0)

    def down(x):
        return jnp.where(row == 0, 0.0, pltpu.roll(x, 1, 0))

    def up(x):
        return jnp.where(row == last, 0.0, pltpu.roll(x, rows - 1, 0))

    def before(x):
        return pltpu.roll(x, 1, 1)

    def after(x):
        return pltpu.roll(x, nlon - 1, 1)

    def fold(x):
        total = x[0:8]
        for i in range(8, rows, 8):
            total = total + x[i:i + 8]
        return total

    def levels(body):
        lax.fori_loop(0, lev, lambda l, c: (body(l), c)[1], 0)

    loads["rs"].wait()
    for l in range(lev):
        rim[0, l:l + 1, :] = rs[l, 0:1, :]
        rim[1, l:l + 1, :] = rs[l, last:rows, :]
    tm_send(3, rim, rim_next)
    for l in range(lev):
        tm_send(4 + l, rs.at[l], lam_next.at[l])
    loads["mv"].wait()

    def _(l):
        z = mv[l] * rs[l]
        zl[l] = z
        acc[0, l] = fold(z * rs[l])
        acc[1, l] = fold(z * z)
        acc[2, l] = jnp.zeros((8, nlon), jnp.float32)
        acc[3, l] = jnp.zeros((8, nlon), jnp.float32)
    levels(_)
    tm_send(1, zl, zl_next)

    @pl.when(jnp.logical_not(has_next))
    def _():
        rim_next[...] = jnp.zeros_like(rim_next)
        lam_next[...] = jnp.zeros_like(lam_next)
        zl_next[...] = jnp.zeros_like(zl_next)

    def mask(j, l):
        return mk[j, l].astype(jnp.float32)

    for name in ("mk", "ro", "wn", "we"):
        loads[name, steps - 1].wait()
    def first_row(side, i, l):
        j = steps - 1
        seen = mk[j, l, i:i + 1, :].astype(jnp.float32)
        return seen * ro[j, l, i:i + 1, :] - rim_next[side, l:l + 1, :]

    def send_adjoint(slot, t, j):
        def _(l):
            if slot == 0:
                lo, hi = first_row(0, 0, l), first_row(1, last, l)
            else:
                lo, hi = t[l, 0:1, :], t[l, last:rows, :]
            stage_lo[slot, pl.ds(l, 1), :] = KAPPA * lo + 0.5 * (wn[j, l, 0:1, :] * lo)
            stage_hi[slot, pl.ds(l, 1), :] = KAPPA * hi - 0.5 * (wn[j, l, last:rows, :] * hi)
        for l in range(lev):
            _(l)
        start(slot)

    def send_forward(slot, s):
        for l in range(lev):
            stage_lo[slot, pl.ds(l, 1), :] = s[l, 0:1, :]
            stage_hi[slot, pl.ds(l, 1), :] = s[l, last:rows, :]
        start(slot)

    def start(slot):
        @pl.when(has_lo)
        def _():
            to_lo(slot, sp - 1).start()

        @pl.when(has_hi)
        def _():
            to_hi(slot, sp + 1).start()

    def finish(slot, t, j=None):
        @pl.when(has_lo)
        def _():
            to_hi(slot, sp - 1).wait_recv()
            for l in range(lev):
                got = recv_lo[slot, pl.ds(l, 1), :]
                if j is not None:
                    got = (KAPPA + 0.5 * wn[j, l, 0:1, :]) * got
                t[l, 0:1, :] = t[l, 0:1, :] + got

        @pl.when(has_hi)
        def _():
            to_lo(slot, sp + 1).wait_recv()
            for l in range(lev):
                got = recv_hi[slot, pl.ds(l, 1), :]
                if j is not None:
                    got = (KAPPA - 0.5 * wn[j, l, last:rows, :]) * got
                t[l, last:rows, :] = t[l, last:rows, :] + got

    def transposed(t, j, l):
        x = t[l]
        k = KAPPA * x
        e = 0.5 * (we[j, l] * x)
        n = 0.5 * (wn[j, l] * x)
        return (1.0 - 4.0 * KAPPA) * x + before(k - e) + after(k + e) + down(k - n) + up(k + n)

    def adjoint1(j):
        if j > 0:
            def _(l):
                if j == steps - 1:
                    tm_recv(4 + l, rs.at[l], lam_next.at[l])
                    t1[l] = mask(j, l) * ro[j, l] - lam_next[l]
                t1[l] = transposed(t1, j, l) + mask(j - 1, l) * ro[j - 1, l]
        else:
            def _(l):
                zdx[l] = transposed(t1, j, l) + rs[l]
        levels(_)

    def inject2(j, l):
        z = ov[j, l] * ro[j, l]
        acc[0, l] += fold(z * ro[j, l])
        acc[1, l] += fold(z * z)
        return mask(j, l) * z

    def adjoint2(j):
        if j > 0:
            def _(l):
                t2[l] = transposed(t2, j, l) + inject2(j - 1, l)
        else:
            def _(l):
                t2[l] = transposed(t2, j, l) + zl[l]
        levels(_)

    def observed(j, l, s):
        z = ov[j, l] * ro[j, l]
        w = ov[j, l] * z + mask(j, l) * s
        acc[2, l] += fold(z * w)
        acc[3, l] += fold(w * w)

    def forward(src, j):
        def _(l):
            x = src[l]
            if j > 0:
                observed(j - 1, l, x)
            else:
                acc[1, l] += fold(x * x)
                u[l] = mv[l] * zl[l] + x
            e, w = after(x), before(x)
            n, s = up(x), down(x)
            st[l] = (
                x
                - 0.5 * (we[j, l] * (e - w))
                - 0.5 * (wn[j, l] * (n - s))
                + KAPPA * (e + w + n + s - 4.0 * x)
            )
        levels(_)

    def start2():
        for j in reversed(range(steps)):
            loads["ov", j].wait()
        tm_recv(1, zl, zl_next)

        def _(l):
            t2[l] = inject2(steps - 1, l) - zl_next[l]
        levels(_)

    def round2(q):
        j = steps - 1 - q
        if q == 0:
            start2()
        else:
            finish(2 * steps + q - 1, t2)
        if q < steps:
            send_adjoint(2 * steps + q, t2, j)
            adjoint2(j)

    def own_window():
        @pl.when(jnp.logical_not(has_prev))
        def _():
            def _(l):
                acc[2, l] += fold(zl[l] * u[l])
                acc[3, l] += fold(u[l] * u[l])
            levels(_)

    def increments():
        def _(l):
            acc[2, l] += fold(zdx[l] * t2[l])
            acc[3, l] += fold(t2[l] * t2[l])
        levels(_)

    lag = steps // 2
    for r in range(2 * steps):
        if r < steps:
            j = steps - 1 - r
            if r == 0:
                tm_recv(3, rim, rim_next)
            send_adjoint(r, t1, j)
            if j > 0:
                for name in ("mk", "ro", "wn", "we"):
                    loads[name, j - 1].wait()
            adjoint1(j)
            target = t1 if j > 0 else zdx
            weight = None
        else:
            j = r - steps
            src = zdx if j == 0 else st
            send_forward(r, src)
            if j == 0:
                out = pltpu.make_async_copy(zdx, zdx_h, out_sem)
                out.start()
            forward(src, j)
            if j == 0:
                tm_send(2, u, u_next)
            target, weight = st, j
        if lag <= r <= lag + steps:
            round2(r - lag)
        if r == lag + steps:
            increments()
        if r == 2 * steps - 1:
            own_window()
            tm_recv(2, u, u_next)
        finish(r, target, weight)

    def _(l):
        observed(steps - 1, l, st[l])
    levels(_)

    @pl.when(has_next)
    def _():
        def _(l):
            w = u_next[l] - st[l]
            acc[2, l] += fold(zl_next[l] * w)
            acc[3, l] += fold(w * w)
        levels(_)

    for i in range(4):
        total = acc[i, 0]
        for l in range(1, lev):
            total = total + acc[i, l]
        lanes = total[:, 0:128]
        for c in range(128, nlon, 128):
            lanes = lanes + total[:, c:c + 128]
        part[0, i:i + 1, :] = jnp.sum(lanes, axis=0, keepdims=True)
    part[0, 4:8, :] = jnp.zeros((4, 128), jnp.float32)

    def gather(count, slots, sends, recvs, device, src):
        copies = [
            pltpu.make_async_remote_copy(
                src_ref=src, dst_ref=slots.at[d - 1],
                send_sem=sends.at[d - 1], recv_sem=recvs.at[d - 1],
                device_id=device(d), device_id_type=MESH,
            )
            for d in range(1, count)
        ]
        for copy in copies:
            copy.start()
        total = src[...]
        for d, copy in enumerate(copies):
            copy.wait_recv()
            total = total + slots[d]
        return total, copies

    copies1 = []
    if flat:
        total, copies2 = gather(total_devices, part_sp, psp_s, psp_r, any_device, part.at[0])
    else:
        total, copies1 = gather(
            ntm, part_tm, ptm_s, ptm_r, lambda d: (lax.rem(tm + d, ntm), sp), part.at[0]
        )
        part[1] = total
        total, copies2 = gather(
            nsp, part_sp, psp_s, psp_r, lambda d: (tm, lax.rem(sp + d, nsp)), part.at[1]
        )
    sums = jnp.broadcast_to(jnp.sum(total, axis=1, keepdims=True), (8, 128))
    n, d, e, f = (sums[i:i + 1, :] for i in range(4))
    first = n / d
    second = first * (first * e - d) / (d - 2.0 * first * e + first * first * f)
    coef_ref[0:1, :] = first + second
    coef_ref[1:2, :] = -(first * second)
    coef_ref[2:8, :] = jnp.zeros((6, 128), jnp.float32)

    for copy in copies1 + copies2:
        copy.wait_send()
    for slot in range(3 * steps):
        @pl.when(has_lo)
        def _(slot=slot):
            to_lo(slot, sp - 1).wait_send()

        @pl.when(has_hi)
        def _(slot=slot):
            to_hi(slot, sp + 1).wait_send()

    @pl.when(has_prev)
    def _():
        tm_copy(3, rim, rim_next, tm - 1).wait_send()
        for l in range(lev):
            tm_copy(4 + l, rs.at[l], lam_next.at[l], tm - 1).wait_send()
        tm_copy(1, zl, zl_next, tm - 1).wait_send()
        tm_copy(2, u, u_next, tm - 1).wait_send()
    out.wait()


def combine(coef_h, zdx_h, rs, ro, mv, ov, lam_h, mu_h, dx_h, lam, mu, dx, coef, zdx, sem, in_sem):
    get_coef = pltpu.make_async_copy(coef_h, coef, in_sem.at[0])
    get_zdx = pltpu.make_async_copy(zdx_h, zdx, in_sem.at[1])
    get_coef.start()
    get_zdx.start()
    get_coef.wait()
    steps, lev, rows, nlon = ro.shape
    both = jnp.broadcast_to(coef[0:1, 0:1], (rows, nlon))
    cross = jnp.broadcast_to(coef[1:2, 0:1], (rows, nlon))
    copies = []

    def put(body, src, dst):
        lax.fori_loop(0, lev, lambda l, c: (body(l), c)[1], 0)
        copy = pltpu.make_async_copy(src, dst, sem.at[len(copies)])
        copy.start()
        copies.append(copy)

    for j in range(steps):
        def _(l, j=j):
            mu[j, l] = (both + cross * ov[j, l]) * ro[j, l]
        put(_, mu.at[j], mu_h.at[j])

    def _(l):
        lam[l] = (both + cross * mv[l]) * rs[l]
    put(_, lam, lam_h)

    get_zdx.wait()

    def _(l):
        dx[l] = cross * zdx[l]
    put(_, dx, dx_h)
    for copy in copies:
        copy.wait()


def on_device(ntm, nsp, *args):
    rhs_state, rhs_obs, wind_east, wind_north, model_var, obs_var, obs_mask = (a[0] for a in args)
    steps, lev, rows, nlon = rhs_obs.shape
    f32 = jnp.float32
    field = pltpu.VMEM((lev, rows, nlon), f32)
    fields = pltpu.VMEM((steps, lev, rows, nlon), f32)
    slots = 3 * steps
    far = ntm * nsp - 1 if ntm * nsp <= 64 else nsp - 1
    halo = pltpu.VMEM((slots, lev, nlon), f32)
    rim = pltpu.VMEM((2, lev, nlon), f32)
    dma = pltpu.SemaphoreType.DMA
    hbm = pl.BlockSpec(memory_space=pl.ANY)
    zdx, coef = pl.pallas_call(
        functools.partial(kernel, ntm, nsp),
        out_shape=(
            jax.ShapeDtypeStruct((lev, rows, nlon), f32),
            jax.ShapeDtypeStruct((8, 128), f32),
        ),
        in_specs=[hbm] * 7,
        out_specs=(hbm, pl.BlockSpec(memory_space=pltpu.VMEM)),
        scratch_shapes=[
            field, fields, fields, fields, field, fields,
            pltpu.VMEM((steps, lev, rows, nlon), jnp.int32),
            field, field, field, field, field, field,
            field, field, field, rim, rim,
            pltpu.VMEM((4, lev, 8, nlon), f32), halo, halo, halo, halo,
            pltpu.VMEM((2, 8, 128), f32),
            pltpu.VMEM((ntm - 1, 8, 128), f32),
            pltpu.VMEM((far, 8, 128), f32),
            dma((2 + 5 * steps,)), dma((slots,)), dma((slots,)), dma((slots,)), dma((slots,)),
            dma((4 + lev,)), dma((4 + lev,)),
            dma((ntm - 1,)), dma((ntm - 1,)), dma((far,)), dma((far,)), dma,
        ],
        compiler_params=pltpu.CompilerParams(
            collective_id=0, has_side_effects=True, vmem_limit_bytes=54656 * 1024
        ),
    )(rhs_state, rhs_obs, wind_east, wind_north, model_var, obs_var, obs_mask)
    vmem = pl.BlockSpec(memory_space=pltpu.VMEM)
    lam, mu, dx = pl.pallas_call(
        combine,
        out_shape=(
            jax.ShapeDtypeStruct((lev, rows, nlon), f32),
            jax.ShapeDtypeStruct((steps, lev, rows, nlon), f32),
            jax.ShapeDtypeStruct((lev, rows, nlon), f32),
        ),
        in_specs=[hbm] * 2 + [vmem] * 4,
        out_specs=(hbm, hbm, hbm),
        scratch_shapes=[
            field, fields, field, pltpu.VMEM((8, 128), f32), field, dma((steps + 2,)), dma((2,)),
        ],
        compiler_params=pltpu.CompilerParams(vmem_limit_bytes=16 * 1024 * 1024),
    )(coef, zdx, rhs_state, rhs_obs, model_var, obs_var)
    return lam[None], mu[None], dx[None]


def solution(mesh):
    flat = P("tm", None, "space", None)
    deep = P("tm", None, None, "space", None)
    return jax.shard_map(
        functools.partial(on_device, mesh.shape["tm"], mesh.shape["space"]),
        mesh=mesh,
        in_specs=(flat, deep, deep, deep, flat, deep, deep),
        out_specs=(flat, deep, flat),
        check_vma=False,
    )
```
